128 devices in a mesh: pipe: 8 (over z, y_lo), expert: 16 (over x, y_hi, core).
Axes of the slice: x: 4, y: 4 (y_hi: 2, y_lo: 2; y = y_hi * 2 + y_lo), z: 4, core: 2. Of those that a mesh axis runs over, the one named last changes fastest.
Arguments:
- stream: bfloat16 [2, 256, 3584], P(None, 'expert', 'pipe'), may hold values from -6 to 6
- layer_gain: float32 [8, 3584], P('pipe'), may hold values from 0.5 to 1.5
- router_weight: bfloat16 [8, 3584, 16], P('pipe'), may hold values from -0.09375 to 0.09375
- gate_weight: bfloat16 [8, 16, 3584, 1024], P('pipe', 'expert'), may hold values from -0.09375 to 0.09375
- up_weight: bfloat16 [8, 16, 3584, 1024], P('pipe', 'expert'), may hold values from -0.09375 to 0.09375
- down_weight: bfloat16 [8, 16, 1024, 3584], P('pipe', 'expert'), may hold values from -0.1875 to 0.1875
- routes: int32 [8, 2, 256, 8], P('pipe', None, 'expert'), may hold values from 0 to 15, all different within a row; in each aligned block of 16 rows (0 to 15, 16 to 31, ..., all dimensions but the last counted through in order) at most 8 rows name the same one
- final_gain: float32 [3584], replicated, may hold values from 0.5 to 1.5
- head_weight: bfloat16 [65536, 3584], P(('pipe', 'expert'))
- targets: int32 [2, 256], replicated, may hold values from 0 to 65535
Outputs:
- loss: float32 [2, 256], replicated
The draws below stay inside these ranges and needn't reach their ends.
Inputs may be any that keep to these rules, and one draw needn't show every extreme that they name: `routes`: each token names 8 different experts. Among the 16 tokens of one index of expert in one micro-batch and layer, no expert is named by more than 8 tokens, a bound that some block reaches.
All inputs are finite; a program needn't handle non-finite values.
Results may differ from the reference program's by a relative error of at most 0.013.
Values may be sent and summed in bfloat16 or wider, within the bound.
A program may use at most 128 MiB of HBM per device.

```python
import math
import jax
import jax.numpy as jnp
import numpy as np
from jax import lax

D = 3584
F = 1024
TOP = 8
MICRO = 2
TOK_DEV = 16
VDEV = 512
EXPERTS = 16
LAYERS = 8
TOKENS = 256
CAP = 8
VOCAB = 65536
N_EXPERT = 16


def draw_head_weight(key, part):
    key = jax.random.fold_in(key, 7)
    base_key = jax.random.fold_in(key, 0)
    values = jax.random.normal(base_key, (VOCAB, D), jnp.float32) * (4.0 / math.sqrt(D))
    return values.astype(jnp.bfloat16)


def plant(drawn, rng, low, largest):
    spot = [jax.random.randint(jax.random.fold_in(rng, axis), (), 0, length) for axis, length in enumerate(drawn.shape)]
    main_axis = drawn.shape.index(max(drawn.shape))
    next_to = spot[:main_axis] + [(spot[main_axis] + 1) % drawn.shape[main_axis]] + spot[main_axis + 1:]
    return drawn.at[tuple(spot)].set(low).at[tuple(next_to)].set(largest)


def shard_levels(key, shape, shards, low, largest):
    level = 1.0
    for dim, blocks in shards:
        heights = jax.random.uniform(jax.random.fold_in(jax.random.fold_in(key, 6), dim), (blocks,), jnp.float32, low / len(shards), largest / len(shards))
        level = level * jnp.repeat(jnp.exp(heights), shape[dim] // blocks).reshape((-1,) + (1,) * (len(shape) - 1 - dim))
    return level


def deal_out(rng, own, number, rows, count, top, limit, skew):
    order = jax.random.permutation(rng, count)
    crowded, common = portions_of(count, rows * top, limit, skew, True), portions_of(count, rows * top, limit, skew, False)
    places = jnp.arange(count)

    def named(sizes, turn):
        used = int((sizes > 0).sum())
        fixed = max(1, used // 4)
        shifted = fixed + (places - fixed + turn * (used - fixed)) % max(1, count - fixed)
        return jnp.zeros((count,), jnp.int32).at[order[jnp.where(places < fixed, places, shifted)]].set(jnp.asarray(sizes, jnp.int32))

    sizes = jnp.where(number % 4 == 0, named(crowded, number // 4), named(common, number - number // 4 - 1))
    mixed = jax.random.permutation(jax.random.fold_in(own, 3), count)
    giver, sink = mixed[0:count // 2 * 2:2], mixed[1:count // 2 * 2:2]
    room = jnp.minimum(sizes[giver] - 1, limit - sizes[sink]) // 2
    room = jnp.where((giver == order[0]) | (sink == order[0]) | (sizes[sink] == 0), 0, jnp.maximum(room, 0))
    shifted = jax.random.randint(jax.random.fold_in(own, 4), (count // 2,), 0, 1 << 20) % (room + 1)
    sizes = sizes.at[giver].add(-shifted).at[sink].add(shifted)
    members = jnp.searchsorted(jnp.cumsum(sizes), jnp.arange(rows * top), side="right").astype(jnp.int32)
    table = members.reshape(top, rows).T
    table = table[jax.random.permutation(jax.random.fold_in(own, 1), rows)]
    turn = jax.random.randint(jax.random.fold_in(own, 2), (rows, 1), 0, top)
    return jnp.take_along_axis(table, (jnp.arange(top)[None, :] + turn) % top, axis=1)


def portions_of(amount, total, reach, lean, full):
    portions = [(1 << 20) // math.isqrt(standing ** lean) + 1 for standing in range(1, amount + 1)]
    largest = reach if full else min(reach, max(-(-total // amount), total * portions[0] // sum(portions)))
    least = 1 if total - largest >= amount - 1 else 0
    holding, surplus = [largest] + [least] * (amount - 1), total - largest - least * (amount - 1)
    while surplus > 0:
        candidates = [i for i in range(1, amount) if holding[i] < largest] or [i for i in range(1, amount) if holding[i] < reach]
        whole, left = sum([portions[i] for i in candidates]), surplus
        for i in candidates:
            extra = min(reach - holding[i], max(1, left * portions[i] // whole), surplus)
            holding[i] = holding[i] + extra
            surplus = surplus - extra
    return np.array(holding)


def gaussian(own_key, shape, spread, bound, shards=(), kind=jnp.bfloat16):
    level = shard_levels(own_key, shape, shards, -0.22, 0.18) if shards else 1.0
    array = jax.random.normal(own_key, shape, jnp.float32) * spread * level
    return jnp.minimum(jnp.maximum(array, -bound), bound).astype(kind)


def setup_inputs(seed: int = 0) -> dict:
    streams_of = jax.random.split(jax.random.key(seed), 11)
    stream = gaussian(streams_of[0], (MICRO, TOKENS, D), 1.0, 6.0, ((1, 16), (2, 8)))
    layer_gain = jnp.clip(1.0 + 0.1 * jax.random.normal(streams_of[1], (LAYERS, D), jnp.float32), 0.5, 1.5)
    router_weight = gaussian(streams_of[2], (LAYERS, D, EXPERTS), D ** -0.5, 0.09375, ((0, 8),))
    gate_weight = gaussian(streams_of[3], (LAYERS, EXPERTS, D, F), D ** -0.5, 0.09375, ((0, 8), (1, 16)))
    up_weight = gaussian(streams_of[4], (LAYERS, EXPERTS, D, F), D ** -0.5, 0.09375, ((0, 8), (1, 16)))
    down_weight = gaussian(streams_of[5], (LAYERS, EXPERTS, F, D), F ** -0.5, 0.1875, ((0, 8), (1, 16)))
    routes_keys = jax.random.split(jax.random.fold_in(streams_of[6], 1), LAYERS * MICRO * TOKENS // TOK_DEV)
    routes_turns = jax.random.permutation(jax.random.fold_in(streams_of[6], 3), LAYERS * MICRO * TOKENS // TOK_DEV)
    routes = jax.vmap(lambda own, number: deal_out(jax.random.fold_in(streams_of[6], 2), own, number, TOK_DEV, EXPERTS, TOP, CAP, 1))(routes_keys, routes_turns).reshape((LAYERS, MICRO, TOKENS, TOP))
    final_gain = jnp.clip(1.0 + 0.1 * jax.random.normal(streams_of[7], (D,), jnp.float32), 0.5, 1.5)
    head_weight = draw_head_weight(jax.random.fold_in(streams_of[10], 71), 0)
    targets = plant(jax.random.randint(streams_of[9], (MICRO, TOKENS), 0, VOCAB), jax.random.fold_in(streams_of[9], 1), 0, VOCAB - 1).astype(jnp.int32)
    return dict(stream=stream, layer_gain=layer_gain, router_weight=router_weight, gate_weight=gate_weight, up_weight=up_weight, down_weight=down_weight, routes=routes, final_gain=final_gain, head_weight=head_weight, targets=targets)


routed_scale = 2.5
norm_eps = 1e-06

def slot_tables(route, experts, capacity):
    flat_routes = route.reshape(-1).astype(jnp.int32)
    count = flat_routes.shape[0]
    fanout = route.shape[1]
    one_hot = (flat_routes[:, None] == jnp.arange(experts, dtype=jnp.int32)[None, :]).astype(jnp.int32)
    before = jnp.cumsum(one_hot, axis=0) - one_hot
    place = lax.optimization_barrier(jnp.sum(before * one_hot, axis=1))
    backward = (flat_routes * capacity + place).astype(jnp.int32)
    match = backward[None, :] == jnp.arange(experts * capacity, dtype=jnp.int32)[:, None]
    valid = jnp.any(match, axis=1)
    source = lax.optimization_barrier(jnp.sum(jnp.where(match, jnp.arange(count, dtype=jnp.int32)[None, :] // fanout, 0), axis=1))
    return (source.astype(jnp.int32), valid, backward)

def scaled_norm(value, gain):
    widened = value.astype(jnp.float32)
    inverse = lax.rsqrt(lax.optimization_barrier(jnp.mean(widened * widened, axis=-1, keepdims=True)) + norm_eps)
    return (widened * inverse * gain).astype(jnp.bfloat16)

def route_weights(normed, router, route):
    affinity = jax.nn.sigmoid(jnp.dot(normed, router, preferred_element_type=jnp.float32))
    picked = route[:, :, None] == jnp.arange(router.shape[1], dtype=jnp.int32)[None, None, :]
    chosen = lax.optimization_barrier(jnp.sum(jnp.where(picked, affinity[:, None, :], 0.0), axis=-1))
    return routed_scale * chosen / lax.optimization_barrier(jnp.sum(chosen, axis=-1, keepdims=True))

def expert_rows(rows, w_gate, w_up, w_down):
    gated = jnp.dot(rows, w_gate, preferred_element_type=jnp.float32)
    lifted = jnp.dot(rows, w_up, preferred_element_type=jnp.float32)
    hidden = (jax.nn.silu(gated) * lifted).astype(jnp.bfloat16)
    return jnp.dot(hidden, w_down, preferred_element_type=jnp.float32).astype(jnp.bfloat16)

def one_layer(value, route, gain, router, w_gate, w_up, w_down):
    width = value.shape[1]
    sources = N_EXPERT
    experts = router.shape[1]
    normed = scaled_norm(value, gain)
    weights = route_weights(normed, router, route)
    normed_blocks = normed.reshape(sources, TOK_DEV, width)
    route_blocks = route.reshape(sources, TOK_DEV, route.shape[1])

    def pack(block, block_route):
        source, valid, backward = slot_tables(block_route, experts, CAP)
        rows = jnp.take(block, source, axis=0)
        rows = jnp.where(valid[:, None], rows, jnp.zeros_like(rows))
        return (rows.reshape(experts, CAP, width), backward)
    sent, backward = jax.vmap(pack)(normed_blocks, route_blocks)
    incoming = jnp.transpose(sent, (1, 0, 2, 3)).reshape(experts, sources * CAP, width)

    def run_expert(operands):
        rows, w_one, u_one, d_one = operands
        return expert_rows(rows, w_one, u_one, d_one)
    produced = lax.map(run_expert, (incoming, w_gate, w_up, w_down))
    returned = jnp.transpose(produced.reshape(experts, sources, CAP, width), (1, 0, 2, 3))
    returned = returned.reshape(sources, experts * CAP, width)
    collected = jax.vmap(lambda table, where_from: jnp.take(table, where_from, axis=0))(returned, backward)
    collected = collected.reshape(value.shape[0], route.shape[1], width).astype(jnp.float32)
    mixed = jnp.einsum('tk,tkd->td', weights, collected)
    return (value.astype(jnp.float32) + mixed).astype(jnp.bfloat16)

def reference(stream, layer_gain, router_weight, gate_weight, up_weight, down_weight, routes, final_gain, head_weight, targets):
    states = [stream[index] for index in range(MICRO)]
    for layer in range(LAYERS):
        states = [one_layer(states[index], routes[layer, index], layer_gain[layer], router_weight[layer], gate_weight[layer], up_weight[layer], down_weight[layer]) for index in range(MICRO)]
    drafted = scaled_norm(jnp.stack(states, axis=0), final_gain).reshape(-1, stream.shape[2])
    wanted = targets.reshape(-1).astype(jnp.int32)
    blocks = head_weight.shape[0] // VDEV
    head_blocks = head_weight.reshape(blocks, VDEV, head_weight.shape[1])
    offsets = jnp.arange(blocks, dtype=jnp.int32) * VDEV

    def block_stats(operands):
        table, offset = operands
        logits = lax.dot_general(drafted, table, (((1,), (1,)), ((), ())), preferred_element_type=jnp.float32)
        highest = lax.optimization_barrier(jnp.max(logits, axis=1))
        total = lax.optimization_barrier(jnp.sum(jnp.exp(logits - highest[:, None]), axis=1))
        columns = jnp.arange(VDEV, dtype=jnp.int32)[None, :] + offset
        hit = lax.optimization_barrier(jnp.sum(jnp.where(columns == wanted[:, None], logits, 0.0), axis=1))
        return (highest, total, hit)
    highest, total, hit = lax.map(block_stats, (head_blocks, offsets))
    overall = lax.optimization_barrier(jnp.max(highest, axis=0))
    summed = lax.optimization_barrier(jnp.sum(total * jnp.exp(highest - overall[None, :]), axis=0))
    loss = overall + jnp.log(summed) - lax.optimization_barrier(jnp.sum(hit, axis=0))
    return loss.reshape(targets.shape)
```

```python
import functools

import jax
import jax.numpy as jnp
from jax import lax
from jax.experimental import pallas as pl
from jax.experimental.pallas import tpu as pltpu
from jax.sharding import PartitionSpec as P

routed_scale = 2.5
norm_eps = 1e-06
MESH = pl.DeviceIdType.MESH
f32 = jnp.float32
bf16 = jnp.bfloat16


def iota(shape, axis):
    return lax.broadcasted_iota(jnp.int32, shape, axis)


def dot(a, b):
    return jnp.dot(a, b, preferred_element_type=f32)


def dot_nt(a, b):
    return lax.dot_general(a, b, (((1,), (1,)), ((), ())), preferred_element_type=f32)


def kernel(
    sections,
    experts,
    stream,
    gain,
    router,
    w_gate,
    w_up,
    w_down,
    routes,
    final_gain,
    head,
    targets,
    loss,
    vg,
    vu,
    vd,
    vh,
    gath,
    xin,
    packed,
    recv,
    prod,
    ret,
    hidden,
    rows_in,
    hop,
    fin,
    dall,
    logits,
    spread,
    fold,
    stat,
    stat_pipe,
    stat_mid,
    stat_all,
    w_sem,
    head_sem,
    head_send,
    head_recv,
    stream_send,
    stream_recv,
    disp_send,
    disp_recv,
    back_send,
    back_recv,
    hop_send,
    hop_recv,
    fin_send,
    fin_recv,
    dall_send,
    dall_recv,
    stat_send,
    stat_recv,
):
    micros, tok, part = stream.shape
    half = xin.shape[2]
    width = 2 * half
    cap = 8
    pairs = experts // 2
    slots = experts * cap
    vdev = head.shape[0]
    p = lax.axis_index("pipe")
    e = lax.axis_index("expert")
    chip = e // 2
    core = lax.rem(e, 2)
    last = sections - 1

    def local(src, dst, sem):
        return pltpu.make_async_copy(src, dst, sem)

    def to(src, dst, send, recv_, device):
        return pltpu.make_async_remote_copy(
            src_ref=src, dst_ref=dst, send_sem=send, recv_sem=recv_, device_id=device, device_id_type=MESH
        )

    def drain(ref, sem):
        pltpu.make_async_copy(ref, ref, sem).wait()

    def other_expert(k):
        return lax.rem(e + k, experts)

    def other_section(k):
        return lax.rem(p + k, sections)

    def other_chip(k):
        return 2 * lax.rem(chip + k, pairs) + core

    def each(count, body):
        def step(k, carry):
            body(k)
            return carry

        lax.fori_loop(1, count, step, 0)

    weights = [
        local(w_gate, vg, w_sem.at[0]),
        local(w_up, vu, w_sem.at[1]),
        local(w_down, vd, w_sem.at[2]),
    ]
    for copy in weights:
        copy.start()
    own_head = local(head, vh.at[core], head_sem)
    own_head.start()

    barrier = pltpu.get_barrier_semaphore()

    def greet(device):
        pl.semaphore_signal(barrier, inc=1, device_id=device, device_id_type=MESH)

    each(experts, lambda k: greet((p, other_expert(k))))
    each(sections, lambda k: greet((other_section(k), e)))
    pl.semaphore_wait(barrier, experts + sections - 2)

    stream_out = to(stream, gath.at[p], stream_send, stream_recv, (0, e))

    @pl.when(p > 0)
    def _():
        stream_out.start()

    @pl.when(p == 0)
    def _():
        local(stream, gath.at[0], stream_recv).start()

    head_out = to(head, vh.at[core], head_send, head_recv, (p, 2 * chip + 1 - core))
    head_out.start()

    expert_of = (iota((experts, 2 * slots), 1) // (2 * cap) == iota((experts, 2 * slots), 0)).astype(bf16)
    expert_of_t = (iota((2 * slots, experts), 0) // (2 * cap) == iota((2 * slots, experts), 1)).astype(bf16)
    earlier = (iota((tok, tok), 1) < iota((tok, tok), 0)).astype(bf16)

    def tables(m):
        route = routes[m]
        member = jnp.zeros((tok, experts), f32)
        for k in range(route.shape[1]):
            member = member + (route[:, k : k + 1] == iota((tok, experts), 1)).astype(f32)
        place = dot(earlier, member.astype(bf16))
        code = jnp.where(member > 0, place, -1.0).astype(bf16)
        return member, code

    for m in range(micros):
        member, code = tables(m)
        chosen = dot_nt(expert_of_t, code)
        row = iota((2 * slots, tok), 0)
        valid = chosen == lax.rem(row, cap).astype(f32)
        side = lax.rem(row // cap, 2)
        spread[m] = jnp.concatenate(
            [(valid & (side == 0)).astype(bf16), (valid & (side == 1)).astype(bf16)], axis=1
        )

    gather_row = iota((2 * slots, 2 * slots), 0)
    gather_col = iota((2 * slots, 2 * slots), 1)

    def interleaved(index):
        side = index // slots
        source = lax.rem(index, slots) // cap
        return source * 2 * cap + side * cap + lax.rem(index, cap)

    apart = (interleaved(gather_row) == gather_col).astype(bf16)
    together = (interleaved(gather_col) == gather_row).astype(bf16)

    @pl.when(p == 0)
    def _():
        drain(gath, stream_recv)
        per = sections // 2
        for m in range(micros):
            for side in range(2):
                for j in range(per):
                    xin[m, side * tok : (side + 1) * tok, j * part : (j + 1) * part] = gath[side * per + j, m]

    def normed_of(value, gain_ref):
        wide = value.astype(f32)
        square = jnp.sum(wide * wide, axis=1, keepdims=True)
        mean = (square[:tok] + square[tok:]) / width
        inverse = lax.rsqrt(mean + norm_eps)
        first = wide[:tok] * inverse * gain_ref[:, :half]
        second = wide[tok:] * inverse * gain_ref[:, half:]
        return jnp.concatenate([first, second], axis=0).astype(bf16)

    def dispatch(m):
        @pl.when(p > 0)
        def _():
            drain(xin.at[m], hop_recv.at[m])

        normed = normed_of(xin[m], gain)
        packed[m] = dot(spread[m], normed).astype(bf16)

        def send(k):
            peer = other_expert(k)
            to(
                packed.at[m, pl.ds(pl.multiple_of(peer * 2 * cap, 16), 2 * cap)],
                recv.at[m, pl.ds(pl.multiple_of(e * 2 * cap, 16), 2 * cap)],
                disp_send.at[m],
                disp_recv.at[m],
                (p, peer),
            ).start()

        each(experts, send)
        mine = pl.ds(pl.multiple_of(e * 2 * cap, 16), 2 * cap)
        local(packed.at[m, mine], recv.at[m, mine], disp_recv.at[m]).start()
        member, code = tables(m)
        affinity = jax.nn.sigmoid(dot(normed[:tok], router[:half]) + dot(normed[tok:], router[half:])) * member
        weight = routed_scale * affinity / jnp.sum(affinity, axis=1, keepdims=True)
        upper = weight.astype(bf16)
        lower = (weight - upper.astype(f32)).astype(bf16)
        chosen = dot(code, expert_of)
        column = iota((tok, 2 * slots), 1)
        valid = chosen == lax.rem(column, cap).astype(f32)
        side = lax.rem(column // cap, 2)
        upper = dot(upper, expert_of)
        lower = dot(lower, expert_of)
        one = valid & (side == 0)
        two = valid & (side == 1)
        fold[m] = jnp.concatenate(
            [jnp.where(one, upper, 0.0), jnp.where(two, upper, 0.0), jnp.where(one, lower, 0.0), jnp.where(two, lower, 0.0)],
            axis=0,
        ).astype(bf16)

    def expert_work(m):
        drain(recv.at[m], disp_recv.at[m])
        if m == 0:
            for copy in weights:
                copy.wait()
        rows_in[...] = dot(apart, recv[m]).astype(bf16)
        tile = min(256, hidden.shape[1])

        def up(n, carry):
            cols = pl.ds(pl.multiple_of(n * tile, tile), tile)
            gated = dot(rows_in[:slots], vg[:half, cols]) + dot(rows_in[slots:], vg[half:, cols])
            lifted = dot(rows_in[:slots], vu[:half, cols]) + dot(rows_in[slots:], vu[half:, cols])
            hidden[:, cols] = (gated / (1.0 + jnp.exp(-gated)) * lifted).astype(bf16)
            return carry

        lax.fori_loop(0, hidden.shape[1] // tile, up, 0)

        def down(n, carry):
            first = pl.ds(pl.multiple_of(n * tile, 128), tile)
            second = pl.ds(pl.multiple_of(half + n * tile, 128), tile)
            both = jnp.concatenate([dot(hidden[...], vd[:, first]), dot(hidden[...], vd[:, second])], axis=0)
            prod[m, :, first] = dot(together, both.astype(bf16)).astype(bf16)
            return carry

        lax.fori_loop(0, half // tile, down, 0)

        def send(k):
            peer = other_expert(k)
            to(
                prod.at[m, pl.ds(pl.multiple_of(peer * 2 * cap, 16), 2 * cap)],
                ret.at[m, pl.ds(pl.multiple_of(e * 2 * cap, 16), 2 * cap)],
                back_send.at[m],
                back_recv.at[m],
                (p, peer),
            ).start()

        each(experts, send)
        mine = pl.ds(pl.multiple_of(e * 2 * cap, 16), 2 * cap)
        local(prod.at[m, mine], ret.at[m, mine], back_recv.at[m]).start()

    def combine(m):
        drain(ret.at[m], back_recv.at[m])
        mixed = dot(fold[m], ret[m])
        out = (xin[m].astype(f32) + mixed[: 2 * tok] + mixed[2 * tok :]).astype(bf16)

        @pl.when(p < last)
        def _():
            hop[m] = out
            to(hop.at[m], xin.at[m], hop_send.at[m], hop_recv.at[m], (p + 1, e)).start()

        @pl.when(p == last)
        def _():
            fin[m] = normed_of(out, final_gain)
            each(
                sections,
                lambda k: to(fin.at[m], fin.at[m], fin_send.at[m], fin_recv.at[m], (other_section(k), e)).start(),
            )

    def share(m):
        @pl.when(p < last)
        def _():
            drain(fin.at[m], fin_recv.at[m])

        each(
            pairs,
            lambda k: to(
                fin.at[m], dall.at[m, chip], dall_send.at[m], dall_recv.at[m], (p, other_chip(k))
            ).start(),
        )
        local(fin.at[m], dall.at[m, chip], dall_recv.at[m]).start()

    def head_work(m):
        drain(dall.at[m], dall_recv.at[m])
        if m == 0:
            own_head.wait()
            head_out.wait()
        states = dall[m].reshape(pairs, 2, tok, half)
        first = states[:, 0].reshape(pairs * tok, half)
        second = states[:, 1].reshape(pairs * tok, half)
        tile = min(256, vdev)
        per = vdev // tile

        def step(n, carry):
            block = vh.at[n // per]
            rows = pl.ds(pl.multiple_of(lax.rem(n, per) * tile, tile), tile)
            value = dot_nt(block[rows, :half], first) + dot_nt(block[rows, half:], second)
            logits[pl.ds(pl.multiple_of(n * tile, tile), tile)] = value
            return carry

        lax.fori_loop(0, 2 * per, step, 0)
        value = logits[...]
        highest = jnp.max(value, axis=0, keepdims=True)
        total = jnp.sum(jnp.exp(value - highest), axis=0, keepdims=True)
        entry = iota(value.shape, 0) + (p * experts + 2 * chip) * vdev
        hit = jnp.sum(jnp.where(entry == targets[core, m][None, :], value, 0.0), axis=0, keepdims=True)
        stat[:, m * pairs * tok : (m + 1) * pairs * tok] = jnp.concatenate(
            [highest, total, hit, jnp.zeros((5, pairs * tok), f32)], axis=0
        )

    dispatch(0)
    expert_work(0)
    dispatch(1)
    combine(0)

    @pl.when(p == last)
    def _():
        share(0)

    expert_work(1)
    combine(1)

    @pl.when(p < last)
    def _():
        share(0)

    head_work(0)
    share(1)
    head_work(1)

    def merged(parts):
        highest = functools.reduce(jnp.maximum, [part_[0:1] for part_ in parts])
        total = sum(part_[1:2] * jnp.exp(part_[0:1] - highest) for part_ in parts)
        hit = sum(part_[2:3] for part_ in parts)
        return highest, total, hit

    each(
        sections,
        lambda k: to(stat, stat_pipe.at[p], stat_send.at[0], stat_recv.at[0], (other_section(k), e)).start(),
    )
    local(stat, stat_pipe.at[p], stat_recv.at[0]).start()
    drain(stat_pipe, stat_recv.at[0])
    highest, total, hit = merged([stat_pipe[j] for j in range(sections)])
    stat_mid[...] = jnp.concatenate([highest, total, hit, jnp.zeros((5, highest.shape[1]), f32)], axis=0)
    each(
        experts,
        lambda k: to(stat_mid, stat_all.at[e], stat_send.at[1], stat_recv.at[1], (p, other_expert(k))).start(),
    )
    local(stat_mid, stat_all.at[e], stat_recv.at[1]).start()
    drain(stat_all, stat_recv.at[1])
    for c in range(2):
        highest, total, hit = merged([stat_all[2 * j + c] for j in range(pairs)])
        loss[c : c + 1, :] = highest + jnp.log(total) - hit

    @pl.when(p > 0)
    def _():
        drain(stream, stream_send)

    for m in range(micros):
        for buffer, sem in ((packed, disp_send), (prod, back_send)):
            drain(buffer.at[m, pl.ds(0, 2 * slots - 2 * cap)], sem.at[m])

        @pl.when(p < last)
        def _():
            drain(hop.at[m], hop_send.at[m])

        @pl.when(p == last)
        def _():
            for _ in range(sections - 1):
                drain(fin.at[m], fin_send.at[m])

        drain(dall.at[m, pl.ds(0, pairs - 1)], dall_send.at[m])
    drain(stat_pipe.at[pl.ds(0, sections - 1)], stat_send.at[0])
    drain(stat_all.at[pl.ds(0, experts - 1)], stat_send.at[1])


def local(
    stream,
    layer_gain,
    router_weight,
    gate_weight,
    up_weight,
    down_weight,
    routes,
    final_gain,
    head_weight,
    targets,
):
    sections = lax.axis_size("pipe")
    experts = lax.axis_size("expert")
    micros, tok, part = stream.shape
    width = layer_gain.shape[1]
    half = width // 2
    hidden = gate_weight.shape[3]
    vdev = head_weight.shape[0]
    pairs = experts // 2
    slots = experts * 8
    by_core = targets.reshape(micros, pairs, 2, tok).transpose(2, 0, 1, 3).reshape(2, micros, pairs * tok)
    dma = pltpu.SemaphoreType.DMA
    vmem = pl.BlockSpec(memory_space=pltpu.VMEM)
    hbm = pl.BlockSpec(memory_space=pl.ANY)
    loss = pl.pallas_call(
        functools.partial(kernel, sections, experts),
        out_shape=jax.ShapeDtypeStruct((2, micros * pairs * tok), f32),
        in_specs=[hbm, vmem, vmem, hbm, hbm, hbm, vmem, vmem, hbm, vmem],
        out_specs=vmem,
        scratch_shapes=[
            pltpu.VMEM((width, hidden), bf16),
            pltpu.VMEM((width, hidden), bf16),
            pltpu.VMEM((hidden, width), bf16),
            pltpu.VMEM((2, vdev, width), bf16),
            pltpu.VMEM((sections, micros, tok, part), bf16),
            pltpu.VMEM((micros, 2 * tok, half), bf16),
            pltpu.VMEM((micros, 2 * slots, half), bf16),
            pltpu.VMEM((micros, 2 * slots, half), bf16),
            pltpu.VMEM((micros, 2 * slots, half), bf16),
            pltpu.VMEM((micros, 2 * slots, half), bf16),
            pltpu.VMEM((slots, hidden), bf16),
            pltpu.VMEM((2 * slots, half), bf16),
            pltpu.VMEM((micros, 2 * tok, half), bf16),
            pltpu.VMEM((micros, 2 * tok, half), bf16),
            pltpu.VMEM((micros, pairs, 2 * tok, half), bf16),
            pltpu.VMEM((2 * vdev, pairs * tok), f32),
            pltpu.VMEM((micros, 2 * slots, 2 * tok), bf16),
            pltpu.VMEM((micros, 4 * tok, 2 * slots), bf16),
            pltpu.VMEM((8, micros * pairs * tok), f32),
            pltpu.VMEM((sections, 8, micros * pairs * tok), f32),
            pltpu.VMEM((8, micros * pairs * tok), f32),
            pltpu.VMEM((experts, 8, micros * pairs * tok), f32),
            dma((3,)),
            dma,
            dma,
            dma,
            dma,
            dma,
            dma((micros,)),
            dma((micros,)),
            dma((micros,)),
            dma((micros,)),
            dma((micros,)),
            dma((micros,)),
            dma((micros,)),
            dma((micros,)),
            dma((micros,)),
            dma((micros,)),
            dma((2,)),
            dma((2,)),
        ],
        compiler_params=pltpu.CompilerParams(
            collective_id=0, has_side_effects=True, vmem_limit_bytes=56 * 1024 * 1024
        ),
        name="relay",
    )(
        stream,
        layer_gain,
        router_weight[0],
        gate_weight[0, 0],
        up_weight[0, 0],
        down_weight[0, 0],
        routes[0],
        final_gain[None],
        head_weight,
        by_core,
    )
    loss = loss.reshape(2, micros, pairs, tok).transpose(1, 2, 0, 3)
    return loss.reshape(targets.shape)


def solution(mesh):
    in_specs = (
        P(None, "expert", "pipe"),
        P("pipe", None),
        P("pipe", None, None),
        P("pipe", "expert", None, None),
        P("pipe", "expert", None, None),
        P("pipe", "expert", None, None),
        P("pipe", None, "expert", None),
        P(),
        P(("pipe", "expert"), None),
        P(),
    )
    out_specs = P()
    return jax.shard_map(local, mesh=mesh, in_specs=in_specs, out_specs=out_specs, check_vma=False)
```

```python
import functools

import jax
import jax.numpy as jnp
from jax import lax
from jax.experimental import pallas as pl
from jax.experimental.pallas import tpu as pltpu
from jax.sharding import PartitionSpec as P

routed_scale = 2.5
norm_eps = 1e-06
MESH = pl.DeviceIdType.MESH
f32 = jnp.float32
bf16 = jnp.bfloat16


def iota(shape, axis):
    return lax.broadcasted_iota(jnp.int32, shape, axis)


def dot(a, b):
    return jnp.dot(a, b, preferred_element_type=f32)


def dot_nt(a, b):
    return lax.dot_general(a, b, (((1,), (1,)), ((), ())), preferred_element_type=f32)


def dot_tn(a, b):
    return lax.dot_general(a, b, (((0,), (0,)), ((), ())), preferred_element_type=f32)


def kernel(
    sections,
    experts,
    stream,
    gain,
    router,
    w_gate,
    w_up,
    w_down,
    routes,
    final_gain,
    head,
    targets,
    loss,
    vg,
    vu,
    vd,
    vh,
    gath,
    xin,
    xcur,
    packed,
    recv,
    prod,
    ret,
    hidden,
    rows_in,
    rows_out,
    fin,
    dall,
    logits,
    spread,
    fold,
    fold_in,
    stat,
    stat_pipe,
    stat_mid,
    stat_all,
    w_sem,
    head_sem,
    head_send,
    head_recv,
    stream_send,
    stream_recv,
    disp_send,
    disp_recv,
    back_send,
    back_recv,
    hop_send,
    hop_recv,
    fold_send,
    fold_recv,
    fin_send,
    fin_recv,
    dall_send,
    dall_recv,
    stat_send,
    stat_recv,
):
    micros, tok, part = stream.shape
    half = xin.shape[2]
    width = 2 * half
    cap = 8
    block = 2 * cap
    pairs = experts // 2
    slots = experts * cap
    vdev = head.shape[0]
    p = lax.axis_index("pipe")
    e = lax.axis_index("expert")
    chip = e // 2
    core = lax.rem(e, 2)
    odd = lax.rem(p, 2)
    last = sections - 1

    def local(src, dst, sem):
        return pltpu.make_async_copy(src, dst, sem)

    def to(src, dst, send, recv_, device):
        return pltpu.make_async_remote_copy(
            src_ref=src, dst_ref=dst, send_sem=send, recv_sem=recv_, device_id=device, device_id_type=MESH
        )

    def drain(ref, sem):
        pltpu.make_async_copy(ref, ref, sem).wait()

    def other_expert(k):
        return lax.rem(e + k, experts)

    def other_section(k):
        return lax.rem(p + k, sections)

    def other_chip(k):
        return lax.rem(chip + k, pairs)

    def rows_of(index):
        return pl.ds(pl.multiple_of(index * block, block), block)

    def each(count, body, start=1):
        def step(k, carry):
            body(k)
            return carry

        lax.fori_loop(start, count, step, 0)

    weights = [
        local(w_gate, vg, w_sem.at[0]),
        local(w_up, vu, w_sem.at[1]),
        local(w_down, vd, w_sem.at[2]),
    ]
    for copy in weights:
        copy.start()
    own_head = local(head, vh.at[core], head_sem)
    own_head.start()

    barrier = pltpu.get_barrier_semaphore()

    def greet(device):
        pl.semaphore_signal(barrier, inc=1, device_id=device, device_id_type=MESH)

    partner = p + 1 - 2 * odd
    each(sections, lambda k: greet((other_section(k), e)))
    each(experts, lambda k: greet((p, other_expert(k))))
    each(experts, lambda k: greet((partner, other_expert(k))))
    pl.semaphore_wait(barrier, 2 * (experts - 1) + sections - 1)

    stream_out = to(stream, gath.at[p], stream_send, stream_recv, (0, e))

    @pl.when(p > 0)
    def _():
        stream_out.start()

    @pl.when(p == 0)
    def _():
        local(stream, gath.at[0], stream_recv).start()

    head_out = to(head, vh.at[core], head_send, head_recv, (p, 2 * chip + 1 - core))
    head_out.start()

    expert_of = (iota((experts, 2 * slots), 1) // block == iota((experts, 2 * slots), 0)).astype(bf16)
    expert_of_t = (iota((2 * slots, experts), 0) // block == iota((2 * slots, experts), 1)).astype(bf16)
    earlier = (iota((tok, tok), 0) < iota((tok, tok), 1)).astype(bf16)

    def tables(m):
        route = routes[m]
        member = jnp.zeros((experts, tok), f32)
        for k in range(route.shape[0]):
            member = member + (route[k : k + 1, :] == iota((experts, tok), 0)).astype(f32)
        place = dot(member.astype(bf16), earlier)
        code = jnp.where(member > 0, place, -1.0).astype(bf16)
        return member, code

    for m in range(micros):
        member, code = tables(m)
        chosen = dot(expert_of_t, code)
        row = iota((2 * slots, tok), 0)
        valid = chosen == lax.rem(row, cap).astype(f32)
        side = lax.rem(row // cap, 2)
        spread[m] = jnp.concatenate(
            [(valid & (side == 0)).astype(bf16), (valid & (side == 1)).astype(bf16)], axis=1
        )

    gather_row = iota((slots, slots), 0)
    gather_col = iota((slots, slots), 1)

    def interleaved(index):
        side = index // (slots // 2)
        source = lax.rem(index, slots // 2) // cap
        return source * block + side * cap + lax.rem(index, cap)

    apart = (interleaved(gather_row) == gather_col).astype(bf16)
    together = (interleaved(gather_col) == gather_row).astype(bf16)

    @pl.when(p == 0)
    def _():
        drain(gath, stream_recv)
        per = sections // 2
        for m in range(micros):
            for side in range(2):
                for j in range(per):
                    xin[m, side * tok : (side + 1) * tok, j * part : (j + 1) * part] = gath[side * per + j, m]

    def normed_of(value, first_gain, second_gain):
        wide = value.astype(f32)
        square = jnp.sum(wide * wide, axis=1, keepdims=True)
        mean = (square[:tok] + square[tok:]) / width
        inverse = lax.rsqrt(mean + norm_eps)
        first = wide[:tok] * inverse * first_gain
        second = wide[tok:] * inverse * second_gain
        return jnp.concatenate([first, second], axis=0).astype(bf16)

    def mixed(value, weights_, blocks):
        out = dot(weights_, blocks)
        return (value.astype(f32) + out[: 2 * tok] + out[2 * tok :]).astype(bf16)

    def dispatch(m):
        @pl.when(p > 0)
        def _():
            drain(xin.at[m], hop_recv.at[m])

        @pl.when(odd == 1)
        def _():
            drain(fold_in.at[m], fold_recv.at[m])
            drain(ret.at[0, m], back_recv.at[0, m])
            xcur[m] = mixed(xin[m], fold_in[m], ret[0, m])

        @pl.when(odd == 0)
        def _():
            xcur[m] = xin[m]

        normed = normed_of(xcur[m], gain[:, :half], gain[:, half:])
        packed[m] = dot(spread[m], normed).astype(bf16)

        def send(k):
            peer = other_expert(k)
            to(
                packed.at[m, rows_of(peer)],
                recv.at[m, core, rows_of(chip)],
                disp_send.at[m],
                disp_recv.at[m, core],
                (p, peer),
            ).start()

        each(experts, send)
        local(packed.at[m, rows_of(e)], recv.at[m, core, rows_of(chip)], disp_recv.at[m, core]).start()
        member, code = tables(m)
        affinity = dot_nt(router[:, :half], normed[:tok]) + dot_nt(router[:, half:], normed[tok:])
        affinity = jax.nn.sigmoid(affinity) * member
        weight = routed_scale * affinity / jnp.sum(affinity, axis=0, keepdims=True)
        upper = weight.astype(bf16)
        lower = (weight - upper.astype(f32)).astype(bf16)
        chosen = dot_tn(code, expert_of)
        column = iota((tok, 2 * slots), 1)
        valid = chosen == lax.rem(column, cap).astype(f32)
        side = lax.rem(column // cap, 2)
        upper = dot_tn(upper, expert_of)
        lower = dot_tn(lower, expert_of)
        one = valid & (side == 0)
        two = valid & (side == 1)
        fold[m] = jnp.concatenate(
            [jnp.where(one, upper, 0.0), jnp.where(two, upper, 0.0), jnp.where(one, lower, 0.0), jnp.where(two, lower, 0.0)],
            axis=0,
        ).astype(bf16)

        @pl.when(odd == 0)
        def _():
            to(xin.at[m], xin.at[m], hop_send.at[m], hop_recv.at[m], (p + 1, e)).start()
            to(fold.at[m], fold_in.at[m], fold_send.at[m], fold_recv.at[m], (p + 1, e)).start()

    def expert_work(m, c):
        drain(recv.at[m, c], disp_recv.at[m, c])
        if m == 0 and c == 0:
            weights[0].wait()
            weights[1].wait()
        rows_in[...] = dot(apart, recv[m, c]).astype(bf16)
        rows = slots // 2
        tile = min(512, hidden.shape[1])

        def up(n, carry):
            cols = pl.ds(pl.multiple_of(n * tile, tile), tile)
            gated = dot(rows_in[:rows], vg[:half, cols]) + dot(rows_in[rows:], vg[half:, cols])
            lifted = dot(rows_in[:rows], vu[:half, cols]) + dot(rows_in[rows:], vu[half:, cols])
            hidden[:, cols] = (gated / (1.0 + jnp.exp(-gated)) * lifted).astype(bf16)
            return carry

        lax.fori_loop(0, hidden.shape[1] // tile, up, 0)
        if m == 0 and c == 0:
            weights[2].wait()
        step = min(256, half)

        def down(n, carry):
            first = pl.ds(pl.multiple_of(n * step, 128), step)
            second = pl.ds(pl.multiple_of(half + n * step, 128), step)
            rows_out[:rows, first] = dot(hidden[...], vd[:, first]).astype(bf16)
            rows_out[rows:, first] = dot(hidden[...], vd[:, second]).astype(bf16)
            return carry

        lax.fori_loop(0, half // step, down, 0)
        prod[m, c] = dot(together, rows_out[...]).astype(bf16)

        def send(k):
            peer = other_chip(k)
            to(
                prod.at[m, c, rows_of(peer)],
                ret.at[odd, m, rows_of(e)],
                back_send.at[m, c],
                back_recv.at[odd, m],
                (p + 1 - odd, 2 * peer + c),
            ).start()

        each(pairs, send)
        here = (odd == 1) & (core == c)

        @pl.when(here)
        def _():
            local(prod.at[m, c, rows_of(chip)], ret.at[1, m, rows_of(e)], back_recv.at[1, m]).start()

        @pl.when(jnp.logical_not(here))
        def _():
            send(0)

    def share(m):
        def send(k):
            peer = 2 * other_chip(k) + core
            to(fin.at[m], dall.at[m, chip], dall_send.at[m], dall_recv.at[m], (p, peer)).start()

        each(pairs, send)
        local(fin.at[m], dall.at[m, chip], dall_recv.at[m]).start()

    def combine(m):
        drain(ret.at[1, m], back_recv.at[1, m])
        out = mixed(xcur[m], fold[m], ret[1, m])

        @pl.when(p < last)
        def _():
            xcur[m] = out
            to(xcur.at[m], xin.at[m], hop_send.at[m], hop_recv.at[m], (p + 1, e)).start()

        @pl.when(p == last)
        def _():
            fin[m] = normed_of(out, final_gain[:half][None], final_gain[half:][None])

            def send(k):
                to(fin.at[m], fin.at[m], fin_send.at[m], fin_recv.at[m], (other_section(k), e)).start()

            each(sections, send)
            share(m)

    def arrive(m):
        @pl.when(p < last)
        def _():
            drain(fin.at[m], fin_recv.at[m])
            share(m)

    def head_work(m):
        drain(dall.at[m], dall_recv.at[m])
        if m == 0:
            own_head.wait()
            head_out.wait()
        states = dall[m].reshape(pairs, 2, tok, half)
        first = states[:, 0].reshape(pairs * tok, half)
        second = states[:, 1].reshape(pairs * tok, half)
        tile = min(256, vdev)
        per = vdev // tile

        def step(n, carry):
            part_ = vh.at[n // per]
            rows = pl.ds(pl.multiple_of(lax.rem(n, per) * tile, tile), tile)
            value = dot_nt(part_[rows, :half], first) + dot_nt(part_[rows, half:], second)
            logits[pl.ds(pl.multiple_of(n * tile, tile), tile)] = value
            return carry

        lax.fori_loop(0, 2 * per, step, 0)
        value = logits[...]
        highest = jnp.max(value, axis=0, keepdims=True)
        total = jnp.sum(jnp.exp(value - highest), axis=0, keepdims=True)
        count = experts * tok
        lane = iota((count, pairs * tok), 1)
        pick = (iota((count, pairs * tok), 0) == (2 * (lane // tok) + core) * tok + lax.rem(lane, tok)).astype(bf16)
        wanted = targets[m : m + 1, :]
        upper = wanted // 256
        lower = wanted - upper * 256
        wanted = 256.0 * dot(upper.astype(f32).astype(bf16), pick) + dot(lower.astype(f32).astype(bf16), pick)
        entry = iota(value.shape, 0) + (p * experts + 2 * chip) * vdev
        hit = jnp.sum(jnp.where(entry.astype(f32) == wanted, value, 0.0), axis=0, keepdims=True)
        stat[:, m * pairs * tok : (m + 1) * pairs * tok] = jnp.concatenate(
            [highest, total, hit, jnp.zeros((5, pairs * tok), f32)], axis=0
        )

    @pl.when(core == 0)
    def _():
        dispatch(0)

    expert_work(0, 0)

    @pl.when(core == 1)
    def _():
        dispatch(0)

    @pl.when((core == 0) & (odd == 1))
    def _():
        combine(0)

    expert_work(0, 1)

    @pl.when(core == 0)
    def _():
        dispatch(1)

    @pl.when((core == 1) & (odd == 1))
    def _():
        combine(0)

    expert_work(1, 0)

    @pl.when(core == 1)
    def _():
        dispatch(1)

    @pl.when((core == 0) & (odd == 1))
    def _():
        combine(1)

    expert_work(1, 1)

    @pl.when((core == 1) & (odd == 1))
    def _():
        combine(1)


    arrive(0)
    head_work(0)
    arrive(1)
    head_work(1)

    def merged(parts):
        highest = functools.reduce(jnp.maximum, [part_[0:1] for part_ in parts])
        total = sum(part_[1:2] * jnp.exp(part_[0:1] - highest) for part_ in parts)
        hit = sum(part_[2:3] for part_ in parts)
        return highest, total, hit

    def send_pipe(k):
        to(stat, stat_pipe.at[p], stat_send.at[0], stat_recv.at[0], (other_section(k), e)).start()

    each(sections, send_pipe)
    local(stat, stat_pipe.at[p], stat_recv.at[0]).start()
    drain(stat_pipe, stat_recv.at[0])
    highest, total, hit = merged([stat_pipe[j] for j in range(sections)])
    stat_mid[...] = jnp.concatenate([highest, total, hit, jnp.zeros((5, highest.shape[1]), f32)], axis=0)

    def send_all(k):
        to(stat_mid, stat_all.at[e], stat_send.at[1], stat_recv.at[1], (p, other_expert(k))).start()

    each(experts, send_all)
    local(stat_mid, stat_all.at[e], stat_recv.at[1]).start()
    drain(stat_all, stat_recv.at[1])
    count = experts * tok
    result = jnp.zeros((micros, count), f32)
    for c in range(2):
        highest, total, hit = merged([stat_all[2 * j + c] for j in range(pairs)])
        value = highest + jnp.log(total) - hit
        value = jnp.concatenate([value[:, m * pairs * tok : (m + 1) * pairs * tok] for m in range(micros)], axis=0)
        lane = iota((pairs * tok, count), 0)
        pick = ((2 * (lane // tok) + c) * tok + lax.rem(lane, tok) == iota((pairs * tok, count), 1)).astype(bf16)
        for _ in range(3):
            piece = value.astype(bf16)
            value = value - piece.astype(f32)
            result = result + dot(piece, pick)
    loss[...] = result

    @pl.when(p > 0)
    def _():
        drain(stream, stream_send)

    for m in range(micros):
        drain(packed.at[m, pl.ds(0, 2 * slots - block)], disp_send.at[m])
        for c in range(2):
            drain(prod.at[m, c, pl.ds(0, slots - block)], back_send.at[m, c])

            @pl.when(jnp.logical_not((odd == 1) & (core == c)))
            def _():
                drain(prod.at[m, c, pl.ds(0, block)], back_send.at[m, c])

        @pl.when(p < last)
        def _():
            drain(xin.at[m], hop_send.at[m])

        @pl.when(odd == 0)
        def _():
            drain(fold.at[m], fold_send.at[m])

        @pl.when(p == last)
        def _():
            for _ in range(sections - 1):
                drain(fin.at[m], fin_send.at[m])

        drain(dall.at[m, pl.ds(0, pairs - 1)], dall_send.at[m])
    drain(stat_pipe.at[pl.ds(0, sections - 1)], stat_send.at[0])
    drain(stat_all.at[pl.ds(0, experts - 1)], stat_send.at[1])


def local(
    stream,
    layer_gain,
    router_weight,
    gate_weight,
    up_weight,
    down_weight,
    routes,
    final_gain,
    head_weight,
    targets,
):
    sections = lax.axis_size("pipe")
    experts = lax.axis_size("expert")
    micros, tok, part = stream.shape
    width = layer_gain.shape[1]
    half = width // 2
    hidden = gate_weight.shape[3]
    vdev = head_weight.shape[0]
    pairs = experts // 2
    slots = experts * 8
    dma = pltpu.SemaphoreType.DMA
    vmem = pl.BlockSpec(memory_space=pltpu.VMEM)
    hbm = pl.BlockSpec(memory_space=pl.ANY)
    return pl.pallas_call(
        functools.partial(kernel, sections, experts),
        out_shape=jax.ShapeDtypeStruct(targets.shape, f32),
        in_specs=[hbm, vmem, vmem, hbm, hbm, hbm, vmem, vmem, hbm, vmem],
        out_specs=vmem,
        scratch_shapes=[
            pltpu.VMEM((width, hidden), bf16),
            pltpu.VMEM((width, hidden), bf16),
            pltpu.VMEM((hidden, width), bf16),
            pltpu.VMEM((2, vdev, width), bf16),
            pltpu.VMEM((sections, micros, tok, part), bf16),
            pltpu.VMEM((micros, 2 * tok, half), bf16),
            pltpu.VMEM((micros, 2 * tok, half), bf16),
            pltpu.VMEM((micros, 2 * slots, half), bf16),
            pltpu.VMEM((micros, 2, slots, half), bf16),
            pltpu.VMEM((micros, 2, slots, half), bf16),
            pltpu.VMEM((2, micros, 2 * slots, half), bf16),
            pltpu.VMEM((slots // 2, hidden), bf16),
            pltpu.VMEM((slots, half), bf16),
            pltpu.VMEM((slots, half), bf16),
            pltpu.VMEM((micros, 2 * tok, half), bf16),
            pltpu.VMEM((micros, pairs, 2 * tok, half), bf16),
            pltpu.VMEM((2 * vdev, pairs * tok), f32),
            pltpu.VMEM((micros, 2 * slots, 2 * tok), bf16),
            pltpu.VMEM((micros, 4 * tok, 2 * slots), bf16),
            pltpu.VMEM((micros, 4 * tok, 2 * slots), bf16),
            pltpu.VMEM((8, micros * pairs * tok), f32),
            pltpu.VMEM((sections, 8, micros * pairs * tok), f32),
            pltpu.VMEM((8, micros * pairs * tok), f32),
            pltpu.VMEM((experts, 8, micros * pairs * tok), f32),
            dma((3,)),
            dma,
            dma,
            dma,
            dma,
            dma,
            dma((micros,)),
            dma((micros, 2)),
            dma((micros, 2)),
            dma((2, micros)),
            dma((micros,)),
            dma((micros,)),
            dma((micros,)),
            dma((micros,)),
            dma((micros,)),
            dma((micros,)),
            dma((micros,)),
            dma((micros,)),
            dma((2,)),
            dma((2,)),
        ],
        compiler_params=pltpu.CompilerParams(
            collective_id=0, has_side_effects=True, vmem_limit_bytes=56 * 1024 * 1024
        ),
        name="relay",
    )(
        stream,
        layer_gain,
        router_weight[0].T,
        gate_weight[0, 0],
        up_weight[0, 0],
        down_weight[0, 0],
        jnp.swapaxes(routes[0], 1, 2),
        final_gain,
        head_weight,
        targets,
    )


def solution(mesh):
    in_specs = (
        P(None, "expert", "pipe"),
        P("pipe", None),
        P("pipe", None, None),
        P("pipe", "expert", None, None),
        P("pipe", "expert", None, None),
        P("pipe", "expert", None, None),
        P("pipe", None, "expert", None),
        P(),
        P(("pipe", "expert"), None),
        P(),
    )
    out_specs = P()
    return jax.shard_map(local, mesh=mesh, in_specs=in_specs, out_specs=out_specs, check_vma=False)
```

```python
import functools

import jax
import jax.numpy as jnp
from jax import lax
from jax.experimental import pallas as pl
from jax.experimental.pallas import tpu as pltpu
from jax.sharding import PartitionSpec as P

routed_scale = 2.5
norm_eps = 1e-06
MESH = pl.DeviceIdType.MESH
f32 = jnp.float32
bf16 = jnp.bfloat16


def iota(shape, axis):
    return lax.broadcasted_iota(jnp.int32, shape, axis)


def dot(a, b):
    return jnp.dot(a, b, preferred_element_type=f32)


def dot_nt(a, b):
    return lax.dot_general(a, b, (((1,), (1,)), ((), ())), preferred_element_type=f32)


def dot_tn(a, b):
    return lax.dot_general(a, b, (((0,), (0,)), ((), ())), preferred_element_type=f32)


def kernel(
    sections,
    experts,
    stream,
    gain,
    router,
    w_gate,
    w_up,
    w_down,
    routes,
    final_gain,
    head,
    targets,
    loss,
    vg,
    vu,
    vd,
    vh,
    gath,
    xin,
    xcur,
    packed,
    recv,
    prod,
    ret,
    hidden,
    partial,
    fin,
    dall,
    logits,
    spread,
    fold,
    fold_in,
    stat,
    stat_pipe,
    stat_mid,
    stat_all,
    w_sem,
    head_sem,
    head_send,
    head_recv,
    stream_send,
    stream_recv,
    disp_send,
    disp_recv,
    back_send,
    back_recv,
    hop_send,
    hop_recv,
    fold_send,
    fold_recv,
    fin_send,
    fin_recv,
    dall_send,
    dall_recv,
    relay_send,
    stat_send,
    stat_recv,
):
    micros, tok, part = stream.shape
    half = xin.shape[2]
    width = 2 * half
    cap = 8
    block = 2 * cap
    pairs = experts // 2
    slots = experts * cap
    vdev = head.shape[0]
    p = lax.axis_index("pipe")
    e = lax.axis_index("expert")
    chip = e // 2
    core = lax.rem(e, 2)
    odd = lax.rem(p, 2)
    last = sections - 1
    lead = (half * 4 // 7 + 255) // 256 * 256 if half > 512 else half // 2
    pieces = [pl.ds(0, lead), pl.ds(lead, half - lead)]

    def shifted(piece):
        return pl.ds(half + piece.start, piece.size)

    def local(src, dst, sem):
        return pltpu.make_async_copy(src, dst, sem)

    def to(src, dst, send, recv_, device):
        return pltpu.make_async_remote_copy(
            src_ref=src, dst_ref=dst, send_sem=send, recv_sem=recv_, device_id=device, device_id_type=MESH
        )

    def drain(ref, sem):
        pltpu.make_async_copy(ref, ref, sem).wait()

    def other_expert(k):
        return lax.rem(e + k, experts)

    def other_section(k):
        return lax.rem(p + k, sections)

    def other_chip(k):
        return lax.rem(chip + k, pairs)

    def rows_of(index):
        return pl.ds(pl.multiple_of(index * block, block), block)

    def each(count, body, start=1):
        def step(k, carry):
            body(k)
            return carry

        lax.fori_loop(start, count, step, 0)

    weights = [
        local(w_gate, vg, w_sem.at[0]),
        local(w_up, vu, w_sem.at[1]),
        local(w_down, vd, w_sem.at[2]),
    ]
    for copy in weights:
        copy.start()
    own_head = local(head, vh.at[core], head_sem)
    own_head.start()

    barrier = pltpu.get_barrier_semaphore()

    def greet(device):
        pl.semaphore_signal(barrier, inc=1, device_id=device, device_id_type=MESH)

    partner = p + 1 - 2 * odd
    each(sections, lambda k: greet((other_section(k), e)))
    each(experts, lambda k: greet((p, other_expert(k))))
    each(experts, lambda k: greet((partner, other_expert(k))))
    pl.semaphore_wait(barrier, 2 * (experts - 1) + sections - 1)

    stream_out = to(stream, gath.at[p], stream_send, stream_recv, (0, e))

    @pl.when(p > 0)
    def _():
        stream_out.start()

    @pl.when(p == 0)
    def _():
        local(stream, gath.at[0], stream_recv).start()

    head_out = to(head, vh.at[core], head_send, head_recv, (p, 2 * chip + 1 - core))
    head_out.start()

    expert_of = (iota((experts, 2 * slots), 1) // block == iota((experts, 2 * slots), 0)).astype(bf16)
    expert_of_t = (iota((2 * slots, experts), 0) // block == iota((2 * slots, experts), 1)).astype(bf16)
    earlier = (iota((tok, tok), 0) < iota((tok, tok), 1)).astype(bf16)

    def tables(m):
        route = routes[m]
        member = jnp.zeros((experts, tok), f32)
        for k in range(route.shape[0]):
            member = member + (route[k : k + 1, :] == iota((experts, tok), 0)).astype(f32)
        place = dot(member.astype(bf16), earlier)
        code = jnp.where(member > 0, place, -1.0).astype(bf16)
        return member, code

    for m in range(micros):
        member, code = tables(m)
        chosen = dot(expert_of_t, code)
        row = iota((2 * slots, tok), 0)
        valid = chosen == lax.rem(row, cap).astype(f32)
        side = lax.rem(row // cap, 2)
        spread[m] = jnp.concatenate(
            [(valid & (side == 0)).astype(bf16), (valid & (side == 1)).astype(bf16)], axis=1
        )

    gather_row = iota((slots, slots), 0)
    gather_col = iota((slots, slots), 1)

    def interleaved(index):
        side = index // (slots // 2)
        source = lax.rem(index, slots // 2) // cap
        return source * block + side * cap + lax.rem(index, cap)

    apart = (interleaved(gather_row) == gather_col).astype(bf16)
    together = (interleaved(gather_col) == gather_row).astype(bf16)

    @pl.when(p == 0)
    def _():
        drain(gath, stream_recv)
        per = sections // 2
        for m in range(micros):
            for side in range(2):
                for j in range(per):
                    xin[m, side * tok : (side + 1) * tok, j * part : (j + 1) * part] = gath[side * per + j, m]

    def normed_of(value, first_gain, second_gain):
        wide = value.astype(f32)
        square = jnp.sum(wide * wide, axis=1, keepdims=True)
        mean = (square[:tok] + square[tok:]) / width
        inverse = lax.rsqrt(mean + norm_eps)
        first = wide[:tok] * inverse * first_gain
        second = wide[tok:] * inverse * second_gain
        return jnp.concatenate([first, second], axis=0).astype(bf16)

    def mixed(value, weights_, blocks):
        out = dot(weights_, blocks)
        return (value.astype(f32) + out[: 2 * tok] + out[2 * tok :]).astype(bf16)

    def dispatch(m):
        @pl.when(p > 0)
        def _():
            drain(xin.at[m], hop_recv.at[m])

        @pl.when(odd == 1)
        def _():
            drain(fold_in.at[m], fold_recv.at[m])
            for q, cols in enumerate(pieces):
                drain(ret.at[0, m, :, cols], back_recv.at[q, 0, m])
                xcur[m, :, cols] = mixed(xin[m, :, cols], fold_in[m], ret[0, m, :, cols])

        @pl.when(odd == 0)
        def _():
            xcur[m] = xin[m]

        normed = normed_of(xcur[m], gain[:, :half], gain[:, half:])
        for q, cols in enumerate(pieces):
            packed[m, :, cols] = dot(spread[m], normed[:, cols.start : cols.start + cols.size]).astype(bf16)

            def send(k, q=q, cols=cols):
                peer = other_expert(k)
                to(
                    packed.at[m, rows_of(peer), cols],
                    recv.at[m, core, rows_of(chip), cols],
                    disp_send.at[m],
                    disp_recv.at[q, m, core],
                    (p, peer),
                ).start()

            each(experts, send)
            local(
                packed.at[m, rows_of(e), cols], recv.at[m, core, rows_of(chip), cols], disp_recv.at[q, m, core]
            ).start()

        member, code = tables(m)
        affinity = dot_nt(router[:, :half], normed[:tok]) + dot_nt(router[:, half:], normed[tok:])
        affinity = jax.nn.sigmoid(affinity) * member
        weight = routed_scale * affinity / jnp.sum(affinity, axis=0, keepdims=True)
        upper = weight.astype(bf16)
        lower = (weight - upper.astype(f32)).astype(bf16)
        chosen = dot_tn(code, expert_of)
        column = iota((tok, 2 * slots), 1)
        valid = chosen == lax.rem(column, cap).astype(f32)
        side = lax.rem(column // cap, 2)
        upper = dot_tn(upper, expert_of)
        lower = dot_tn(lower, expert_of)
        one = valid & (side == 0)
        two = valid & (side == 1)
        fold[m] = jnp.concatenate(
            [jnp.where(one, upper, 0.0), jnp.where(two, upper, 0.0), jnp.where(one, lower, 0.0), jnp.where(two, lower, 0.0)],
            axis=0,
        ).astype(bf16)

        @pl.when(odd == 0)
        def _():
            to(xin.at[m], xin.at[m], hop_send.at[m], hop_recv.at[m], (p + 1, e)).start()
            to(fold.at[m], fold_in.at[m], fold_send.at[m], fold_recv.at[m], (p + 1, e)).start()

    def expert_work(m, c):
        rows = slots // 2
        tile = min(512, hidden.shape[1])
        for q, cols in enumerate(pieces):
            drain(recv.at[m, c, :, cols], disp_recv.at[q, m, c])
            if q == 0:

                @pl.when((m == 0) & (c == 0))
                def _():
                    weights[0].wait()
                    weights[1].wait()

            given = dot(apart, recv[m, c, :, cols]).astype(bf16)
            second = shifted(cols)
            for n in range(hidden.shape[1] // tile):
                part_ = pl.ds(n * tile, tile)
                gated = dot(given[:rows], vg[cols, part_]) + dot(given[rows:], vg[second, part_])
                lifted = dot(given[:rows], vu[cols, part_]) + dot(given[rows:], vu[second, part_])
                if q == 0:
                    partial[0, :, part_] = gated
                    partial[1, :, part_] = lifted
                else:
                    gated = gated + partial[0, :, part_]
                    lifted = lifted + partial[1, :, part_]
                    hidden[:, part_] = (gated / (1.0 + jnp.exp(-gated)) * lifted).astype(bf16)

        @pl.when((m == 0) & (c == 0))
        def _():
            weights[2].wait()

        here = (odd == 1) & (core == c)
        for q, cols in enumerate(pieces):
            out = jnp.concatenate(
                [dot(hidden[...], vd[:, cols]).astype(bf16), dot(hidden[...], vd[:, shifted(cols)]).astype(bf16)], axis=0
            )
            prod[m, c, :, cols] = dot(together, out).astype(bf16)

            def send(k, q=q, cols=cols):
                peer = other_chip(k)
                to(
                    prod.at[m, c, rows_of(peer), cols],
                    ret.at[odd, m, rows_of(e), cols],
                    back_send.at[m, c],
                    back_recv.at[q, odd, m],
                    (p + 1 - odd, 2 * peer + c),
                ).start()

            each(pairs, send)

            @pl.when(here)
            def _(q=q, cols=cols):
                local(
                    prod.at[m, c, rows_of(chip), cols], ret.at[1, m, rows_of(e), cols], back_recv.at[q, 1, m]
                ).start()

            @pl.when(jnp.logical_not(here))
            def _(send=send):
                send(0)

    def share(m):
        def send(k):
            peer = 2 * other_chip(k) + core
            to(fin.at[m], dall.at[m, chip], dall_send.at[m], dall_recv.at[m], (p, peer)).start()

        each(pairs, send)
        local(fin.at[m], dall.at[m, chip], dall_recv.at[m]).start()

    def combine(m):
        for q, cols in enumerate(pieces):
            drain(ret.at[1, m, :, cols], back_recv.at[q, 1, m])
            xcur[m, :, cols] = mixed(xcur[m, :, cols], fold[m], ret[1, m, :, cols])

            @pl.when(p < last)
            def _(cols=cols):
                to(
                    xcur.at[m, :, cols], xin.at[m, :, cols], hop_send.at[m], hop_recv.at[m], (p + 1, e)
                ).start()

        @pl.when(p == last)
        def _():
            fin[m] = normed_of(xcur[m], final_gain[:half][None], final_gain[half:][None])

            def send(k):
                to(fin.at[m], fin.at[m], fin_send.at[m], fin_recv.at[m], (other_section(k), e)).start()

            each(sections, send)

            @pl.when((m == micros - 1) & (core == 1))
            def _():
                share(m)

    def arrive(m):
        drain(fin.at[m], fin_recv.at[m])

        @pl.when((p < last - 1) | ((m == micros - 1) & (core == 1)))
        def _():
            share(m)

    def relayed(m):
        return (p >= last - 3) & (p < last - 1) & jnp.logical_not((m == micros - 1) & (core == 1))

    def relay_out(m):
        return to(dall.at[m], dall.at[m], relay_send.at[m], dall_recv.at[m], (p + 2, e))

    def head_work(m):
        drain(dall.at[m], dall_recv.at[m])

        @pl.when(relayed(m))
        def _():
            relay_out(m).start()

        @pl.when(m == 0)
        def _():
            own_head.wait()
            head_out.wait()

        states = dall[m].reshape(pairs, 2, tok, half)
        first = states[:, 0].reshape(pairs * tok, half)
        second = states[:, 1].reshape(pairs * tok, half)
        tile = min(256, vdev)
        per = vdev // tile

        def step(n, carry):
            part_ = vh.at[n // per]
            rows = pl.ds(pl.multiple_of(lax.rem(n, per) * tile, tile), tile)
            value = dot_nt(part_[rows, :half], first) + dot_nt(part_[rows, half:], second)
            logits[pl.ds(pl.multiple_of(n * tile, tile), tile)] = value
            return carry

        lax.fori_loop(0, 2 * per, step, 0)
        value = logits[...]
        highest = jnp.max(value, axis=0, keepdims=True)
        total = jnp.sum(jnp.exp(value - highest), axis=0, keepdims=True)
        count = experts * tok
        lane = iota((count, pairs * tok), 1)
        pick = (iota((count, pairs * tok), 0) == (2 * (lane // tok) + core) * tok + lax.rem(lane, tok)).astype(bf16)
        wanted = targets[pl.ds(m, 1), :]
        upper = wanted // 256
        lower = wanted - upper * 256
        wanted = 256.0 * dot(upper.astype(f32).astype(bf16), pick) + dot(lower.astype(f32).astype(bf16), pick)
        entry = iota(value.shape, 0) + (p * experts + 2 * chip) * vdev
        hit = jnp.sum(jnp.where(entry.astype(f32) == wanted, value, 0.0), axis=0, keepdims=True)
        stat[m] = jnp.concatenate(
            [highest, total, hit, jnp.zeros((5, pairs * tok), f32)], axis=0
        )

    def chunk(j, carry):
        m = j // 2
        c = lax.rem(j, 2)

        @pl.when(core == c)
        def _():
            dispatch(m)

        expert_work(m, c)

        @pl.when((core == c) & (odd == 1))
        def _():
            combine(m)

        return carry

    lax.fori_loop(0, 2 * micros, chunk, 0)

    def draft(m, carry):
        @pl.when(p < last)
        def _():
            arrive(m)

        head_work(m)
        return carry

    lax.fori_loop(0, micros, draft, 0)

    def merged(parts):
        highest = functools.reduce(jnp.maximum, [part_[:, 0:1] for part_ in parts])
        total = sum(part_[:, 1:2] * jnp.exp(part_[:, 0:1] - highest) for part_ in parts)
        hit = sum(part_[:, 2:3] for part_ in parts)
        return highest, total, hit

    def send_pipe(k):
        to(stat, stat_pipe.at[p], stat_send.at[0], stat_recv.at[0], (other_section(k), e)).start()

    each(sections, send_pipe)
    local(stat, stat_pipe.at[p], stat_recv.at[0]).start()
    drain(stat_pipe, stat_recv.at[0])
    highest, total, hit = merged([stat_pipe[j] for j in range(sections)])
    stat_mid[...] = jnp.concatenate([highest, total, hit, jnp.zeros((micros, 5, pairs * tok), f32)], axis=1)

    def send_all(k):
        to(stat_mid, stat_all.at[e], stat_send.at[1], stat_recv.at[1], (p, other_expert(k))).start()

    each(experts, send_all)
    local(stat_mid, stat_all.at[e], stat_recv.at[1]).start()
    drain(stat_all, stat_recv.at[1])
    count = experts * tok
    result = jnp.zeros((micros, count), f32)
    for c in range(2):
        highest, total, hit = merged([stat_all[2 * j + c] for j in range(pairs)])
        value = highest + jnp.log(total) - hit
        value = jnp.concatenate([value[m] for m in range(micros)], axis=0)
        lane = iota((pairs * tok, count), 0)
        pick = ((2 * (lane // tok) + c) * tok + lax.rem(lane, tok) == iota((pairs * tok, count), 1)).astype(bf16)
        for _ in range(3):
            piece = value.astype(bf16)
            value = value - piece.astype(f32)
            result = result + dot(piece, pick)
    loss[...] = result

    @pl.when(p > 0)
    def _():
        drain(stream, stream_send)

    for m in range(micros):
        drain(packed.at[m, pl.ds(0, 2 * slots - block)], disp_send.at[m])
        for c in range(2):
            drain(prod.at[m, c, pl.ds(0, slots - block)], back_send.at[m, c])

            @pl.when(jnp.logical_not((odd == 1) & (core == c)))
            def _():
                drain(prod.at[m, c, pl.ds(0, block)], back_send.at[m, c])

        @pl.when(p < last)
        def _():
            drain(xin.at[m], hop_send.at[m])

        @pl.when(odd == 0)
        def _():
            drain(fold.at[m], fold_send.at[m])

        @pl.when(p == last)
        def _():
            for _ in range(sections - 1):
                drain(fin.at[m], fin_send.at[m])

        @pl.when((p < last - 1) | ((m == micros - 1) & (core == 1)))
        def _():
            drain(dall.at[m, pl.ds(0, pairs - 1)], dall_send.at[m])

        @pl.when(relayed(m))
        def _():
            drain(dall.at[m], relay_send.at[m])

    drain(stat_pipe.at[pl.ds(0, sections - 1)], stat_send.at[0])
    drain(stat_all.at[pl.ds(0, experts - 1)], stat_send.at[1])


def local(
    stream,
    layer_gain,
    router_weight,
    gate_weight,
    up_weight,
    down_weight,
    routes,
    final_gain,
    head_weight,
    targets,
):
    sections = lax.axis_size("pipe")
    experts = lax.axis_size("expert")
    micros, tok, part = stream.shape
    width = layer_gain.shape[1]
    half = width // 2
    hidden = gate_weight.shape[3]
    vdev = head_weight.shape[0]
    pairs = experts // 2
    slots = experts * 8
    dma = pltpu.SemaphoreType.DMA
    vmem = pl.BlockSpec(memory_space=pltpu.VMEM)
    hbm = pl.BlockSpec(memory_space=pl.ANY)
    return pl.pallas_call(
        functools.partial(kernel, sections, experts),
        out_shape=jax.ShapeDtypeStruct(targets.shape, f32),
        in_specs=[hbm, vmem, vmem, hbm, hbm, hbm, vmem, vmem, hbm, vmem],
        out_specs=vmem,
        scratch_shapes=[
            pltpu.VMEM((width, hidden), bf16),
            pltpu.VMEM((width, hidden), bf16),
            pltpu.VMEM((hidden, width), bf16),
            pltpu.VMEM((2, vdev, width), bf16),
            pltpu.VMEM((sections, micros, tok, part), bf16),
            pltpu.VMEM((micros, 2 * tok, half), bf16),
            pltpu.VMEM((micros, 2 * tok, half), bf16),
            pltpu.VMEM((micros, 2 * slots, half), bf16),
            pltpu.VMEM((micros, 2, slots, half), bf16),
            pltpu.VMEM((micros, 2, slots, half), bf16),
            pltpu.VMEM((2, micros, 2 * slots, half), bf16),
            pltpu.VMEM((slots // 2, hidden), bf16),
            pltpu.VMEM((2, slots // 2, hidden), f32),
            pltpu.VMEM((micros, 2 * tok, half), bf16),
            pltpu.VMEM((micros, pairs, 2 * tok, half), bf16),
            pltpu.VMEM((2 * vdev, pairs * tok), f32),
            pltpu.VMEM((micros, 2 * slots, 2 * tok), bf16),
            pltpu.VMEM((micros, 4 * tok, 2 * slots), bf16),
            pltpu.VMEM((micros, 4 * tok, 2 * slots), bf16),
            pltpu.VMEM((micros, 8, pairs * tok), f32),
            pltpu.VMEM((sections, micros, 8, pairs * tok), f32),
            pltpu.VMEM((micros, 8, pairs * tok), f32),
            pltpu.VMEM((experts, micros, 8, pairs * tok), f32),
            dma((3,)),
            dma,
            dma,
            dma,
            dma,
            dma,
            dma((micros,)),
            dma((2, micros, 2)),
            dma((micros, 2)),
            dma((2, 2, micros)),
            dma((micros,)),
            dma((micros,)),
            dma((micros,)),
            dma((micros,)),
            dma((micros,)),
            dma((micros,)),
            dma((micros,)),
            dma((micros,)),
            dma((micros,)),
            dma((2,)),
            dma((2,)),
        ],
        compiler_params=pltpu.CompilerParams(
            collective_id=0, has_side_effects=True, vmem_limit_bytes=56 * 1024 * 1024
        ),
        name="relay",
    )(
        stream,
        layer_gain,
        router_weight[0].T,
        gate_weight[0, 0],
        up_weight[0, 0],
        down_weight[0, 0],
        jnp.swapaxes(routes[0], 1, 2),
        final_gain,
        head_weight,
        targets,
    )


def solution(mesh):
    in_specs = (
        P(None, "expert", "pipe"),
        P("pipe", None),
        P("pipe", None, None),
        P("pipe", "expert", None, None),
        P("pipe", "expert", None, None),
        P("pipe", "expert", None, None),
        P("pipe", None, "expert", None),
        P(),
        P(("pipe", "expert"), None),
        P(),
    )
    out_specs = P()
    return jax.shard_map(local, mesh=mesh, in_specs=in_specs, out_specs=out_specs, check_vma=False)
```

```python
import functools

import jax
import jax.numpy as jnp
from jax import lax
from jax.experimental import pallas as pl
from jax.experimental.pallas import tpu as pltpu
from jax.sharding import PartitionSpec as P

routed_scale = 2.5
norm_eps = 1e-06
MESH = pl.DeviceIdType.MESH
f32 = jnp.float32
bf16 = jnp.bfloat16


def iota(shape, axis):
    return lax.broadcasted_iota(jnp.int32, shape, axis)


def dot(a, b):
    return jnp.dot(a, b, preferred_element_type=f32)


def dot_nt(a, b):
    return lax.dot_general(a, b, (((1,), (1,)), ((), ())), preferred_element_type=f32)


def dot_tn(a, b):
    return lax.dot_general(a, b, (((0,), (0,)), ((), ())), preferred_element_type=f32)


def kernel(
    sections,
    experts,
    stream,
    gain,
    router,
    w_gate,
    w_up,
    w_down,
    routes,
    final_gain,
    head,
    targets,
    loss,
    vg,
    vu,
    vd,
    vh,
    gath,
    xin,
    xcur,
    packed,
    recv,
    prod,
    ret,
    hidden,
    partial,
    fin,
    dall,
    logits,
    spread,
    fold,
    fold_in,
    stat,
    stat_pipe,
    stat_mid,
    stat_all,
    w_sem,
    head_sem,
    head_send,
    head_recv,
    stream_send,
    stream_recv,
    disp_send,
    disp_recv,
    back_send,
    back_recv,
    hop_send,
    hop_recv,
    fold_send,
    fold_recv,
    fin_send,
    fin_recv,
    dall_send,
    dall_recv,
    relay_send,
    stat_send,
    stat_recv,
):
    micros, tok, part = stream.shape
    half = xin.shape[2]
    width = 2 * half
    cap = 8
    block = 2 * cap
    pairs = experts // 2
    slots = experts * cap
    vdev = head.shape[0]
    p = lax.axis_index("pipe")
    e = lax.axis_index("expert")
    chip = e // 2
    core = lax.rem(e, 2)
    odd = lax.rem(p, 2)
    last = sections - 1
    lead = (half * 4 // 7 + 255) // 256 * 256 if half > 512 else half // 2
    pieces = [pl.ds(0, lead), pl.ds(lead, half - lead)]

    def shifted(piece):
        return pl.ds(half + piece.start, piece.size)

    def local(src, dst, sem):
        return pltpu.make_async_copy(src, dst, sem)

    def to(src, dst, send, recv_, device):
        return pltpu.make_async_remote_copy(
            src_ref=src, dst_ref=dst, send_sem=send, recv_sem=recv_, device_id=device, device_id_type=MESH
        )

    def drain(ref, sem):
        pltpu.make_async_copy(ref, ref, sem).wait()

    def other_expert(k):
        return lax.rem(e + k, experts)

    def other_section(k):
        return lax.rem(p + k, sections)

    def other_chip(k):
        return lax.rem(chip + k, pairs)

    def rows_of(index):
        return pl.ds(pl.multiple_of(index * block, block), block)

    def each(count, body, start=1):
        def step(k, carry):
            body(k)
            return carry

        lax.fori_loop(start, count, step, 0)

    weights = [
        local(w_gate, vg, w_sem.at[0]),
        local(w_up, vu, w_sem.at[1]),
        local(w_down, vd, w_sem.at[2]),
    ]
    for copy in weights:
        copy.start()
    own_head = local(head, vh.at[core], head_sem)
    own_head.start()

    barrier = pltpu.get_barrier_semaphore()

    def greet(device):
        pl.semaphore_signal(barrier, inc=1, device_id=device, device_id_type=MESH)

    partner = p + 1 - 2 * odd
    each(sections, lambda k: greet((other_section(k), e)))
    each(experts, lambda k: greet((p, other_expert(k))))
    each(experts, lambda k: greet((partner, other_expert(k))))
    pl.semaphore_wait(barrier, 2 * (experts - 1) + sections - 1)

    stream_out = to(stream, gath.at[p], stream_send, stream_recv, (0, e))

    @pl.when(p > 0)
    def _():
        stream_out.start()

    @pl.when(p == 0)
    def _():
        local(stream, gath.at[0], stream_recv).start()

    head_out = to(head, vh.at[core], head_send, head_recv, (p, 2 * chip + 1 - core))
    head_out.start()

    expert_of = (iota((experts, 2 * slots), 1) // block == iota((experts, 2 * slots), 0)).astype(bf16)
    expert_of_t = (iota((2 * slots, experts), 0) // block == iota((2 * slots, experts), 1)).astype(bf16)
    earlier = (iota((tok, tok), 0) < iota((tok, tok), 1)).astype(bf16)

    def tables(m):
        route = routes[m]
        member = jnp.zeros((experts, tok), f32)
        for k in range(route.shape[0]):
            member = member + (route[k : k + 1, :] == iota((experts, tok), 0)).astype(f32)
        place = dot(member.astype(bf16), earlier)
        code = jnp.where(member > 0, place, -1.0).astype(bf16)
        return member, code

    for m in range(micros):
        member, code = tables(m)
        chosen = dot(expert_of_t, code)
        row = iota((2 * slots, tok), 0)
        valid = chosen == lax.rem(row, cap).astype(f32)
        side = lax.rem(row // cap, 2)
        spread[m] = jnp.concatenate(
            [(valid & (side == 0)).astype(bf16), (valid & (side == 1)).astype(bf16)], axis=1
        )

    @pl.when(p == 0)
    def _():
        drain(gath, stream_recv)
        per = sections // 2
        for m in range(micros):
            for side in range(2):
                for j in range(per):
                    xin[m, side * tok : (side + 1) * tok, j * part : (j + 1) * part] = gath[side * per + j, m]

    def normed_of(value, first_gain, second_gain):
        wide = value.astype(f32)
        square = jnp.sum(wide * wide, axis=1, keepdims=True)
        mean = (square[:tok] + square[tok:]) / width
        inverse = lax.rsqrt(mean + norm_eps)
        first = wide[:tok] * inverse * first_gain
        second = wide[tok:] * inverse * second_gain
        return jnp.concatenate([first, second], axis=0).astype(bf16)

    def mixed(value, weights_, blocks):
        out = dot(weights_, blocks)
        return (value.astype(f32) + out[: 2 * tok] + out[2 * tok :]).astype(bf16)

    def dispatch(m):
        @pl.when(p > 0)
        def _():
            drain(xin.at[m], hop_recv.at[m])

        @pl.when(odd == 1)
        def _():
            drain(fold_in.at[m], fold_recv.at[m])
            for q, cols in enumerate(pieces):
                drain(ret.at[0, m, :, cols], back_recv.at[q, 0, m])
                xcur[m, :, cols] = mixed(xin[m, :, cols], fold_in[m], ret[0, m, :, cols])

        @pl.when(odd == 0)
        def _():
            xcur[m] = xin[m]

        normed = normed_of(xcur[m], gain[:, :half], gain[:, half:])
        for q, cols in enumerate(pieces):
            packed[m, :, cols] = dot(spread[m], normed[:, cols.start : cols.start + cols.size]).astype(bf16)

            def send(k, q=q, cols=cols):
                peer = other_expert(k)
                to(
                    packed.at[m, rows_of(peer), cols],
                    recv.at[m, core, rows_of(chip), cols],
                    disp_send.at[m],
                    disp_recv.at[q, m, core],
                    (p, peer),
                ).start()

            each(experts, send)
            local(
                packed.at[m, rows_of(e), cols], recv.at[m, core, rows_of(chip), cols], disp_recv.at[q, m, core]
            ).start()

        member, code = tables(m)
        affinity = dot_nt(router[:, :half], normed[:tok]) + dot_nt(router[:, half:], normed[tok:])
        affinity = jax.nn.sigmoid(affinity) * member
        weight = routed_scale * affinity / jnp.sum(affinity, axis=0, keepdims=True)
        upper = weight.astype(bf16)
        lower = (weight - upper.astype(f32)).astype(bf16)
        chosen = dot_tn(code, expert_of)
        column = iota((tok, 2 * slots), 1)
        valid = chosen == lax.rem(column, cap).astype(f32)
        side = lax.rem(column // cap, 2)
        upper = dot_tn(upper, expert_of)
        lower = dot_tn(lower, expert_of)
        one = valid & (side == 0)
        two = valid & (side == 1)
        fold[m] = jnp.concatenate(
            [jnp.where(one, upper, 0.0), jnp.where(two, upper, 0.0), jnp.where(one, lower, 0.0), jnp.where(two, lower, 0.0)],
            axis=0,
        ).astype(bf16)

        @pl.when(odd == 0)
        def _():
            to(xin.at[m], xin.at[m], hop_send.at[m], hop_recv.at[m], (p + 1, e)).start()
            to(fold.at[m], fold_in.at[m], fold_send.at[m], fold_recv.at[m], (p + 1, e)).start()

    def expert_work(m, c):
        rows = slots // 2
        tile = min(512, hidden.shape[1])
        for q, cols in enumerate(pieces):
            drain(recv.at[m, c, :, cols], disp_recv.at[q, m, c])
            if q == 0:

                @pl.when((m == 0) & (c == 0))
                def _():
                    weights[0].wait()
                    weights[1].wait()

            blocks = recv[m, c, :, cols].astype(f32).reshape(pairs, 2, cap, cols.size)
            one = blocks[:, 0].reshape(rows, cols.size).astype(bf16)
            two = blocks[:, 1].reshape(rows, cols.size).astype(bf16)
            second = shifted(cols)
            for n in range(hidden.shape[1] // tile):
                part_ = pl.ds(n * tile, tile)
                gated = dot(one, vg[cols, part_]) + dot(two, vg[second, part_])
                lifted = dot(one, vu[cols, part_]) + dot(two, vu[second, part_])
                if q == 0:
                    partial[0, :, part_] = gated
                    partial[1, :, part_] = lifted
                else:
                    gated = gated + partial[0, :, part_]
                    lifted = lifted + partial[1, :, part_]
                    hidden[:, part_] = (gated / (1.0 + jnp.exp(-gated)) * lifted).astype(bf16)

        @pl.when((m == 0) & (c == 0))
        def _():
            weights[2].wait()

        here = (odd == 1) & (core == c)
        for q, cols in enumerate(pieces):
            one = dot(hidden[...], vd[:, cols]).reshape(pairs, cap, cols.size)
            two = dot(hidden[...], vd[:, shifted(cols)]).reshape(pairs, cap, cols.size)
            prod[m, c, :, cols] = jnp.concatenate([one, two], axis=1).reshape(slots, cols.size).astype(bf16)

            def send(k, q=q, cols=cols):
                peer = other_chip(k)
                to(
                    prod.at[m, c, rows_of(peer), cols],
                    ret.at[odd, m, rows_of(e), cols],
                    back_send.at[m, c],
                    back_recv.at[q, odd, m],
                    (p + 1 - odd, 2 * peer + c),
                ).start()

            each(pairs, send)

            @pl.when(here)
            def _(q=q, cols=cols):
                local(
                    prod.at[m, c, rows_of(chip), cols], ret.at[1, m, rows_of(e), cols], back_recv.at[q, 1, m]
                ).start()

            @pl.when(jnp.logical_not(here))
            def _(send=send):
                send(0)

    def share(m):
        def send(k):
            peer = 2 * other_chip(k) + core
            to(fin.at[m], dall.at[m, chip], dall_send.at[m], dall_recv.at[m], (p, peer)).start()

        each(pairs, send)
        local(fin.at[m], dall.at[m, chip], dall_recv.at[m]).start()

    def combine(m):
        for q, cols in enumerate(pieces):
            drain(ret.at[1, m, :, cols], back_recv.at[q, 1, m])
            xcur[m, :, cols] = mixed(xcur[m, :, cols], fold[m], ret[1, m, :, cols])

            @pl.when(p < last)
            def _(cols=cols):
                to(
                    xcur.at[m, :, cols], xin.at[m, :, cols], hop_send.at[m], hop_recv.at[m], (p + 1, e)
                ).start()

        @pl.when(p == last)
        def _():
            fin[m] = normed_of(xcur[m], final_gain[:half][None], final_gain[half:][None])

            def send(k):
                to(fin.at[m], fin.at[m], fin_send.at[m], fin_recv.at[m], (other_section(k), e)).start()

            each(sections, send)

            @pl.when((m == micros - 1) & (core == 1))
            def _():
                share(m)

    def arrive(m):
        drain(fin.at[m], fin_recv.at[m])

        @pl.when((p < last - 1) | ((m == micros - 1) & (core == 1)))
        def _():
            share(m)

    def relayed(m):
        return (p >= last - 3) & (p < last - 1) & jnp.logical_not((m == micros - 1) & (core == 1))

    def relay_out(m):
        return to(dall.at[m], dall.at[m], relay_send.at[m], dall_recv.at[m], (p + 2, e))

    def head_work(m):
        drain(dall.at[m], dall_recv.at[m])

        @pl.when(relayed(m))
        def _():
            relay_out(m).start()

        @pl.when(m == 0)
        def _():
            own_head.wait()
            head_out.wait()

        states = dall[m].reshape(pairs, 2, tok, half)
        first = states[:, 0].reshape(pairs * tok, half)
        second = states[:, 1].reshape(pairs * tok, half)
        tile = min(256, vdev)
        per = vdev // tile

        def step(n, carry):
            part_ = vh.at[n // per]
            rows = pl.ds(pl.multiple_of(lax.rem(n, per) * tile, tile), tile)
            value = dot_nt(part_[rows, :half], first) + dot_nt(part_[rows, half:], second)
            logits[pl.ds(pl.multiple_of(n * tile, tile), tile)] = value
            return carry

        lax.fori_loop(0, 2 * per, step, 0)
        value = logits[...]
        highest = jnp.max(value, axis=0, keepdims=True)
        total = jnp.sum(jnp.exp(value - highest), axis=0, keepdims=True)
        count = experts * tok
        lane = iota((count, pairs * tok), 1)
        pick = (iota((count, pairs * tok), 0) == (2 * (lane // tok) + core) * tok + lax.rem(lane, tok)).astype(bf16)
        wanted = targets[pl.ds(m, 1), :]
        upper = wanted // 256
        lower = wanted - upper * 256
        wanted = 256.0 * dot(upper.astype(f32).astype(bf16), pick) + dot(lower.astype(f32).astype(bf16), pick)
        entry = iota(value.shape, 0) + (p * experts + 2 * chip) * vdev
        hit = jnp.sum(jnp.where(entry.astype(f32) == wanted, value, 0.0), axis=0, keepdims=True)
        stat[m] = jnp.concatenate(
            [highest, total, hit, jnp.zeros((5, pairs * tok), f32)], axis=0
        )

    def chunk(j, carry):
        m = j // 2
        c = lax.rem(j, 2)

        @pl.when(core == c)
        def _():
            dispatch(m)

        expert_work(m, c)

        @pl.when((core == c) & (odd == 1))
        def _():
            combine(m)

        return carry

    lax.fori_loop(0, 2 * micros, chunk, 0)

    def draft(m, carry):
        @pl.when(p < last)
        def _():
            arrive(m)

        head_work(m)
        return carry

    lax.fori_loop(0, micros, draft, 0)

    def merged(parts):
        highest = functools.reduce(jnp.maximum, [part_[:, 0:1] for part_ in parts])
        total = sum(part_[:, 1:2] * jnp.exp(part_[:, 0:1] - highest) for part_ in parts)
        hit = sum(part_[:, 2:3] for part_ in parts)
        return highest, total, hit

    def send_pipe(k):
        to(stat, stat_pipe.at[p], stat_send.at[0], stat_recv.at[0], (other_section(k), e)).start()

    each(sections, send_pipe)
    local(stat, stat_pipe.at[p], stat_recv.at[0]).start()
    drain(stat_pipe, stat_recv.at[0])
    highest, total, hit = merged([stat_pipe[j] for j in range(sections)])
    stat_mid[...] = jnp.concatenate([highest, total, hit, jnp.zeros((micros, 5, pairs * tok), f32)], axis=1)

    def send_all(k):
        to(stat_mid, stat_all.at[e], stat_send.at[1], stat_recv.at[1], (p, other_expert(k))).start()

    each(experts, send_all)
    local(stat_mid, stat_all.at[e], stat_recv.at[1]).start()
    drain(stat_all, stat_recv.at[1])
    count = experts * tok
    result = jnp.zeros((micros, count), f32)
    for c in range(2):
        highest, total, hit = merged([stat_all[2 * j + c] for j in range(pairs)])
        value = highest + jnp.log(total) - hit
        value = jnp.concatenate([value[m] for m in range(micros)], axis=0)
        lane = iota((pairs * tok, count), 0)
        pick = ((2 * (lane // tok) + c) * tok + lax.rem(lane, tok) == iota((pairs * tok, count), 1)).astype(bf16)
        for _ in range(3):
            piece = value.astype(bf16)
            value = value - piece.astype(f32)
            result = result + dot(piece, pick)
    loss[...] = result

    @pl.when(p > 0)
    def _():
        drain(stream, stream_send)

    for m in range(micros):
        drain(packed.at[m, pl.ds(0, 2 * slots - block)], disp_send.at[m])
        for c in range(2):
            drain(prod.at[m, c, pl.ds(0, slots - block)], back_send.at[m, c])

            @pl.when(jnp.logical_not((odd == 1) & (core == c)))
            def _():
                drain(prod.at[m, c, pl.ds(0, block)], back_send.at[m, c])

        @pl.when(p < last)
        def _():
            drain(xin.at[m], hop_send.at[m])

        @pl.when(odd == 0)
        def _():
            drain(fold.at[m], fold_send.at[m])

        @pl.when(p == last)
        def _():
            for _ in range(sections - 1):
                drain(fin.at[m], fin_send.at[m])

        @pl.when((p < last - 1) | ((m == micros - 1) & (core == 1)))
        def _():
            drain(dall.at[m, pl.ds(0, pairs - 1)], dall_send.at[m])

        @pl.when(relayed(m))
        def _():
            drain(dall.at[m], relay_send.at[m])

    drain(stat_pipe.at[pl.ds(0, sections - 1)], stat_send.at[0])
    drain(stat_all.at[pl.ds(0, experts - 1)], stat_send.at[1])


def local(
    stream,
    layer_gain,
    router_weight,
    gate_weight,
    up_weight,
    down_weight,
    routes,
    final_gain,
    head_weight,
    targets,
):
    sections = lax.axis_size("pipe")
    experts = lax.axis_size("expert")
    micros, tok, part = stream.shape
    width = layer_gain.shape[1]
    half = width // 2
    hidden = gate_weight.shape[3]
    vdev = head_weight.shape[0]
    pairs = experts // 2
    slots = experts * 8
    dma = pltpu.SemaphoreType.DMA
    vmem = pl.BlockSpec(memory_space=pltpu.VMEM)
    hbm = pl.BlockSpec(memory_space=pl.ANY)
    return pl.pallas_call(
        functools.partial(kernel, sections, experts),
        out_shape=jax.ShapeDtypeStruct(targets.shape, f32),
        in_specs=[hbm, vmem, vmem, hbm, hbm, hbm, vmem, vmem, hbm, vmem],
        out_specs=vmem,
        scratch_shapes=[
            pltpu.VMEM((width, hidden), bf16),
            pltpu.VMEM((width, hidden), bf16),
            pltpu.VMEM((hidden, width), bf16),
            pltpu.VMEM((2, vdev, width), bf16),
            pltpu.VMEM((sections, micros, tok, part), bf16),
            pltpu.VMEM((micros, 2 * tok, half), bf16),
            pltpu.VMEM((micros, 2 * tok, half), bf16),
            pltpu.VMEM((micros, 2 * slots, half), bf16),
            pltpu.VMEM((micros, 2, slots, half), bf16),
            pltpu.VMEM((micros, 2, slots, half), bf16),
            pltpu.VMEM((2, micros, 2 * slots, half), bf16),
            pltpu.VMEM((slots // 2, hidden), bf16),
            pltpu.VMEM((2, slots // 2, hidden), f32),
            pltpu.VMEM((micros, 2 * tok, half), bf16),
            pltpu.VMEM((micros, pairs, 2 * tok, half), bf16),
            pltpu.VMEM((2 * vdev, pairs * tok), f32),
            pltpu.VMEM((micros, 2 * slots, 2 * tok), bf16),
            pltpu.VMEM((micros, 4 * tok, 2 * slots), bf16),
            pltpu.VMEM((micros, 4 * tok, 2 * slots), bf16),
            pltpu.VMEM((micros, 8, pairs * tok), f32),
            pltpu.VMEM((sections, micros, 8, pairs * tok), f32),
            pltpu.VMEM((micros, 8, pairs * tok), f32),
            pltpu.VMEM((experts, micros, 8, pairs * tok), f32),
            dma((3,)),
            dma,
            dma,
            dma,
            dma,
            dma,
            dma((micros,)),
            dma((2, micros, 2)),
            dma((micros, 2)),
            dma((2, 2, micros)),
            dma((micros,)),
            dma((micros,)),
            dma((micros,)),
            dma((micros,)),
            dma((micros,)),
            dma((micros,)),
            dma((micros,)),
            dma((micros,)),
            dma((micros,)),
            dma((2,)),
            dma((2,)),
        ],
        compiler_params=pltpu.CompilerParams(
            collective_id=0, has_side_effects=True, vmem_limit_bytes=56 * 1024 * 1024
        ),
        name="relay",
    )(
        stream,
        layer_gain,
        router_weight[0].T,
        gate_weight[0, 0],
        up_weight[0, 0],
        down_weight[0, 0],
        jnp.swapaxes(routes[0], 1, 2),
        final_gain,
        head_weight,
        targets,
    )


def solution(mesh):
    in_specs = (
        P(None, "expert", "pipe"),
        P("pipe", None),
        P("pipe", None, None),
        P("pipe", "expert", None, None),
        P("pipe", "expert", None, None),
        P("pipe", "expert", None, None),
        P("pipe", None, "expert", None),
        P(),
        P(("pipe", "expert"), None),
        P(),
    )
    out_specs = P()
    return jax.shard_map(local, mesh=mesh, in_specs=in_specs, out_specs=out_specs, check_vma=False)
```
